32 devices in a mesh: var: 4 (over y, x), dp: 8 (over z, core).
Axes of the slice: x: 2, y: 2, z: 4, core: 2. Of those that a mesh axis runs over, the one named last changes fastest.
Arguments:
- fields: bfloat16 [8, 16, 32, 128], P('dp', 'var'), may hold values from -6 to 6
- kernels: bfloat16 [16, 16, 512], P('var'), may hold values from -1.5 to 1.5
- level_map: int32 [16], P('var'), may hold values 0 or 1
- norm_gain_vector: float32 [512], replicated, may hold values from 0.1 to 1.9
- w_in: bfloat16 [512, 2048], replicated, may hold values from -0.25 to 0.25
- w_out: bfloat16 [2048, 512], replicated, may hold values from -0.125 to 0.125
- cotangent: bfloat16 [8, 4, 256, 512], P('dp', None, 'var'), may hold values from -6 to 6
Outputs:
- block_out: bfloat16 [8, 4, 256, 512], P('dp', None, 'var')
- kernel_grad: float32 [16, 16, 512], P('var', None, 'dp')
The draws below stay inside these ranges and needn't reach their ends.
Inputs may be any that keep to these rules, and one draw needn't show every extreme that they name: variable-level v belongs to pressure level v // 4 and enters its aggregate where level_map[v] is 1.
All inputs are finite; a program needn't handle non-finite values. No bound on the sum of `level_map` on one device may be relied on, other than what follows from the above.
Results may differ from the reference program's by a relative error of at most 0.013.
Values may be sent and summed in bfloat16 or wider, within the bound.
A program may use at most 64 MiB of HBM per device.

```python
import jax
import jax.numpy as jnp
from jax import lax

E = 512
F = 2048
PATCH = 4
VAR_DEV = 4
WP = 32
HP = 8
LEVELS = 4
VARS = 16
BATCH = 8
NTOK = 256


def with_ends(drawn, own_key, smallest, high):
    shape = drawn.shape
    place = [jax.random.randint(jax.random.fold_in(own_key, axis), (), 0, shape[axis]) for axis in range(len(shape))]
    drawn = drawn.at[tuple(place)].set(smallest)
    longest = shape.index(max(shape))
    place[longest] = (place[longest] + 1) % shape[longest]
    return drawn.at[tuple(place)].set(high)


def spiked(values, key, source, target, blocks, factor):
    owner, partner = [(jnp.arange(values.shape[dim]) // (values.shape[dim] // blocks)).reshape([-1 if axis == dim else 1 for axis in range(values.ndim)]) for dim in (source, target)]
    chosen = jax.random.permutation(key, blocks)[partner]
    strong = (owner == chosen) | (owner == (partner + blocks // 2) % blocks)
    return jnp.where(strong, factor * values, values)


def steps_of(own_key, extent, cuts, low, largest):
    gain, own = 1.0, jax.random.fold_in(own_key, 6)
    for axis_at, blocks in cuts:
        draws = jnp.exp(jax.random.uniform(jax.random.fold_in(own, axis_at), (blocks,), jnp.float32, low / len(cuts), largest / len(cuts)))
        gain = gain * jnp.repeat(draws, extent[axis_at] // blocks).reshape([-1 if axis == axis_at else 1 for axis in range(len(extent))])
    return gain


def noise(own_key, dims, deviation, reach, pieces=(), kind=jnp.bfloat16):
    loudness = steps_of(own_key, dims, pieces, -0.22, 0.18) if pieces else 1.0
    result = jax.random.normal(own_key, dims, jnp.float32) * deviation * loudness
    return jnp.minimum(jnp.maximum(result, -reach), reach).astype(kind)


def heavy_noise(key, shape, deviation, limit, cuts, heavy, kind=jnp.bfloat16):
    result = deviation * jax.random.normal(key, shape, jnp.float32)
    if cuts:
        result = result * steps_of(key, shape, cuts, -0.22, 0.18)
    return jnp.clip(spiked(result, jax.random.fold_in(key, 3), *heavy), -limit, limit).astype(kind)


def setup_inputs(seed: int = 0) -> dict:
    seeds = jax.random.split(jax.random.key(seed), 8)
    return {
        "fields": noise(seeds[0], (BATCH, VARS, PATCH * HP, PATCH * WP), 1.0, 6.0, ((0, 8), (1, 4))),
        "kernels": noise(seeds[1], (VARS, PATCH * PATCH, E), (PATCH * PATCH) ** -0.5, 1.5, ((0, 4),)),
        "level_map": with_ends((jax.random.randint(seeds[2], (VARS,), 0, 2) < 1).astype(jnp.int32), jax.random.fold_in(seeds[2], 1), 0, 1),
        "norm_gain_vector": jnp.clip(1.0 + 0.18 * jax.random.normal(seeds[3], (E,), jnp.float32), 0.1, 1.9),
        "w_in": noise(seeds[4], (E, F), E ** -0.5, 0.25),
        "w_out": noise(seeds[5], (F, E), F ** -0.5, 0.125),
        "cotangent": heavy_noise(seeds[6], (BATCH, LEVELS, NTOK, E), 1.0, 6.0, ((0, 8), (2, 4)), (0, 3, 8, 2.0)),
    }


def patches_of(image):
    count_v, height, width = image.shape
    shaped = image.reshape(count_v, height // PATCH, PATCH, width // PATCH, PATCH)
    return shaped.transpose(0, 1, 3, 2, 4).reshape(count_v, height // PATCH * (width // PATCH), PATCH * PATCH)

def block_pass(token_rows, grads, norm_gain_vector, w_in, w_out):
    width = token_rows.shape[-1]
    rows = token_rows.reshape(-1, width).astype(jnp.float32)
    mean_row = lax.optimization_barrier(jnp.mean(rows, axis=1, keepdims=True))
    centered_rows = rows - mean_row
    reciprocal_std = lax.rsqrt(lax.optimization_barrier(jnp.mean(centered_rows * centered_rows, axis=1, keepdims=True)) + 1e-05)
    normalized_input = centered_rows * reciprocal_std
    normalized_rows = (normalized_input * norm_gain_vector).astype(jnp.bfloat16)
    pre = jnp.dot(normalized_rows, w_in, preferred_element_type=jnp.float32)
    hidden = jax.nn.gelu(pre, approximate=True).astype(jnp.bfloat16)
    output = (rows + jnp.dot(hidden, w_out, preferred_element_type=jnp.float32)).astype(jnp.bfloat16)
    gradient_rows = grads.reshape(-1, width)
    dhid = jnp.dot(gradient_rows, w_out.T, preferred_element_type=jnp.float32)
    gelu_back = jax.vjp(lambda value: jax.nn.gelu(value, approximate=True), pre)[1]
    dpre = gelu_back(dhid)[0].astype(jnp.bfloat16)
    dnorm = jnp.dot(dpre, w_in.T, preferred_element_type=jnp.float32)
    normalized_gradient = dnorm * norm_gain_vector
    token_gradient = gradient_rows.astype(jnp.float32) + reciprocal_std * (normalized_gradient - lax.optimization_barrier(jnp.mean(normalized_gradient, axis=1, keepdims=True)) - normalized_input * lax.optimization_barrier(jnp.mean(normalized_gradient * normalized_input, axis=1, keepdims=True)))
    return (output.reshape(token_rows.shape), token_gradient.astype(jnp.bfloat16).reshape(token_rows.shape))

def reference(fields, kernels, level_map, norm_gain_vector, w_in, w_out, cotangent):
    count_v = kernels.shape[0]
    level = jnp.arange(count_v, dtype=jnp.int32) // VAR_DEV
    weight = level_map.astype(jnp.float32)
    onehot = (level[None, :] == jnp.arange(LEVELS, dtype=jnp.int32)[:, None]).astype(jnp.float32) * weight[None, :]
    inv = 1.0 / jnp.maximum(lax.optimization_barrier(jnp.sum(onehot, axis=1)), 1.0)
    level_assignment = onehot * inv[:, None]
    level_member = inv[level] * weight
    kernels_flattened = kernels.astype(jnp.float32)

    def one_sample(pair):
        image, grads = pair
        patch_inputs = patches_of(image).astype(jnp.float32)
        patch_embeddings = jnp.einsum('ofm,omt->oft', patch_inputs, kernels_flattened)
        token_rows = jnp.einsum('ab,byd->ayd', level_assignment, patch_embeddings).astype(jnp.bfloat16)
        output, token_gradient = block_pass(token_rows, grads, norm_gain_vector, w_in, w_out)
        variable_gradient = jnp.take(token_gradient, level, axis=0).astype(jnp.float32)
        part = jnp.einsum('cjb,cjz->cbz', patch_inputs, variable_gradient) * level_member[:, None, None]
        return (output, part)
    outputs, parts = lax.map(one_sample, (fields, cotangent))
    scale = float(BATCH * NTOK) ** (-0.5)
    return (outputs, lax.optimization_barrier(jnp.sum(parts, axis=0)) * scale)
```

```python
import functools

import jax
import jax.numpy as jnp
from jax import lax
from jax.experimental import pallas as pl
from jax.experimental.pallas import tpu as pltpu
from jax.sharding import PartitionSpec as P

PATCH = 4
LANES = 128
CHUNKS = 4
MESH = pl.DeviceIdType.MESH
F32 = jnp.float32
BF16 = jnp.bfloat16
GELU_C = 0.7978845608028654
GELU_A = 0.044715


def dot_nn(a, b):
    return lax.dot_general(a, b, (((1,), (0,)), ((), ())), preferred_element_type=F32)


def dot_nt(a, b):
    return lax.dot_general(a, b, (((1,), (1,)), ((), ())), preferred_element_type=F32)


def dot_tn(a, b):
    return lax.dot_general(a, b, (((0,), (0,)), ((), ())), preferred_element_type=F32)


def kernel(
    n_var, n_dp, width, scale, vars_local, wp, hp,
    map_ref, fields_hbm, kernels_hbm, gain_hbm, win_hbm, wout_hbm, cot_hbm,
    out_hbm, kg_ref,
    fields_v, kernels_v, gain_v, win, wout, cot_all, out_all,
    patch32, patch, gprime, gsend, grecv,
    in_sem, win_sem, wout_sem, cot_send, cot_recv, own_sem,
    out_send, out_recv, g_send, g_recv,
):
    my_var = lax.axis_index("var")
    my_dp = lax.axis_index("dp")
    features, hidden_units = win.shape
    step = hidden_units // CHUNKS
    rows = cot_all.shape[1]
    tokens_all = n_var * rows

    barrier = pltpu.get_barrier_semaphore()
    for k in range(1, n_var):
        pl.semaphore_signal(barrier, inc=1, device_id={"var": lax.rem(my_var + k, n_var)}, device_id_type=MESH)
    for k in range(1, n_dp):
        pl.semaphore_signal(barrier, inc=1, device_id={"dp": lax.rem(my_dp + k, n_dp)}, device_id_type=MESH)

    small = [
        pltpu.make_async_copy(fields_hbm, fields_v, in_sem.at[0]),
        pltpu.make_async_copy(kernels_hbm, kernels_v, in_sem.at[1]),
        pltpu.make_async_copy(gain_hbm, gain_v, in_sem.at[2]),
    ]
    for copy in small:
        copy.start()
    win_copies, wout_copies = [], []
    for c in range(CHUNKS):
        part = pl.ds(c * step, step)
        win_copies.append(pltpu.make_async_copy(win_hbm.at[:, part], win.at[:, part], win_sem.at[c]))
        wout_copies.append(pltpu.make_async_copy(wout_hbm.at[part], wout.at[part], wout_sem.at[c]))
        win_copies[c].start()
        wout_copies[c].start()

    pl.semaphore_wait(barrier, n_var - 1 + n_dp - 1)

    cot_copies = []
    for k in range(1, n_var):
        dest = lax.rem(my_var + k, n_var)
        cot_copies.append(pltpu.make_async_remote_copy(
            src_ref=cot_hbm.at[dest], dst_ref=cot_all.at[my_var],
            send_sem=cot_send.at[k], recv_sem=cot_recv.at[k],
            device_id={"var": dest}, device_id_type=MESH))
        cot_copies[-1].start()
    own_cot = pltpu.make_async_copy(cot_hbm.at[my_var], cot_all.at[my_var], own_sem.at[0])
    own_cot.start()

    small[0].wait()
    lines = fields_v.shape[0]
    group = LANES // wp
    per_hp = lines // hp
    r_id = lax.broadcasted_iota(jnp.int32, (LANES, LANES), 0)
    c_id = lax.broadcasted_iota(jnp.int32, (LANES, LANES), 1)
    pick = (r_id == PATCH * (c_id % wp) + c_id // wp).astype(BF16)
    o_id = lax.broadcasted_iota(jnp.int32, (lines, lines), 0)
    i_id = lax.broadcasted_iota(jnp.int32, (lines, lines), 1)
    order = (
        i_id == (hp * PATCH) * ((o_id // PATCH) % vars_local) + PATCH * (o_id // per_hp) + o_id % PATCH
    ).astype(BF16)
    spread = dot_nn(order, dot_nn(fields_v[...], pick).astype(BF16))
    lane_group = lax.broadcasted_iota(jnp.int32, (per_hp, LANES), 1) // wp
    for t in range(hp // group):
        for j in range(PATCH):
            block = None
            for g in range(group):
                source = spread[(group * t + g) * per_hp:(group * t + g + 1) * per_hp, :]
                shift = (wp * (g - j)) % LANES
                moved = pltpu.roll(source, shift, 1) if shift else source
                block = moved if block is None else jnp.where(lane_group == g, moved, block)
            patch32[t, pl.ds(j, per_hp, stride=PATCH), :] = block
        patch[:, t * LANES:(t + 1) * LANES] = patch32[t].astype(BF16)

    weights = [map_ref[v].astype(F32) for v in range(vars_local)]
    count = weights[0]
    for v in range(1, vars_local):
        count = count + weights[v]
    pp = PATCH * PATCH
    inv = 1.0 / jnp.maximum(jnp.full((1, features), count, F32), 1.0)
    row_var = lax.broadcasted_iota(jnp.int32, (vars_local * pp, 1), 0) // pp
    row_weight = jnp.zeros((vars_local * pp, 1), F32)
    for v in range(vars_local):
        row_weight = jnp.where(row_var == v, weights[v], row_weight)
    small[1].wait()
    chosen = (kernels_v[...].astype(F32) * row_weight).astype(BF16)
    tokens = (dot_tn(patch[...], chosen) * inv).astype(BF16).astype(F32)
    mean = jnp.mean(tokens, axis=1, keepdims=True)
    centered = tokens - mean
    rstd = lax.rsqrt(jnp.mean(centered * centered, axis=1, keepdims=True) + 1e-5)
    xhat = centered * rstd
    small[2].wait()
    gain = gain_v[...]
    normed = (xhat * gain).astype(BF16)

    total = tokens
    for c in range(CHUNKS):
        win_copies[c].wait()
        pre = dot_nn(normed, win[:, c * step:(c + 1) * step])
        sq = pre * pre
        half = 0.5 + 0.5 * jnp.tanh(pre * (GELU_C + (GELU_C * GELU_A) * sq))
        hid = pre * half
        gprime[:, c * step:(c + 1) * step] = half + hid * (1.0 - half) * (
            2.0 * GELU_C + (6.0 * GELU_C * GELU_A) * sq)
        wout_copies[c].wait()
        total = total + dot_nn(hid.astype(BF16), wout[c * step:(c + 1) * step, :])
    out_all[...] = total.astype(BF16).reshape(n_var, rows, features)

    out_copies = []
    for k in range(1, n_var):
        dest = lax.rem(my_var + k, n_var)
        out_copies.append(pltpu.make_async_remote_copy(
            src_ref=out_all.at[dest], dst_ref=out_hbm.at[my_var],
            send_sem=out_send.at[k], recv_sem=out_recv.at[k],
            device_id={"var": dest}, device_id_type=MESH))
        out_copies[-1].start()
    own_out = pltpu.make_async_copy(out_all.at[my_var], out_hbm.at[my_var], own_sem.at[1])
    own_out.start()

    own_cot.wait()
    for copy in cot_copies:
        copy.wait()
    cot = cot_all[...].reshape(tokens_all, features)
    dnorm = None
    for c in range(CHUNKS):
        dhid = dot_nt(cot, wout[c * step:(c + 1) * step, :])
        dpre = (dhid * gprime[:, c * step:(c + 1) * step]).astype(BF16)
        term = dot_nt(dpre, win[:, c * step:(c + 1) * step])
        dnorm = term if dnorm is None else dnorm + term
    dx = dnorm * gain
    dtok = cot.astype(F32) + rstd * (
        dx - jnp.mean(dx, axis=1, keepdims=True)
        - xhat * jnp.mean(dx * xhat, axis=1, keepdims=True))
    grad = dot_nn(patch[...], dtok.astype(BF16))

    per_tile = LANES // width
    short = grad.shape[0] // per_tile
    lane_part = lax.broadcasted_iota(jnp.int32, (short, LANES), 1) // width
    for d in range(n_dp):
        tile, j = d // per_tile, d % per_tile
        packed = None
        for g in range(per_tile):
            source = grad[g * short:(g + 1) * short, tile * LANES:(tile + 1) * LANES]
            shift = (width * (g - j)) % LANES
            moved = pltpu.roll(source, shift, 1) if shift else source
            packed = moved if packed is None else jnp.where(lane_part == g, moved, packed)
        gsend[d] = packed.astype(gsend.dtype)
    g_copies = []
    for k in range(1, n_dp):
        dest = lax.rem(my_dp + k, n_dp)
        g_copies.append(pltpu.make_async_remote_copy(
            src_ref=gsend.at[dest], dst_ref=grecv.at[k],
            send_sem=g_send.at[k], recv_sem=g_recv.at[k],
            device_id={"dp": dest}, device_id_type=MESH))
        g_copies[-1].start()
    own_out.wait()
    for copy in out_copies:
        copy.wait()
    summed = gsend[my_dp].astype(F32)
    for k in range(1, n_dp):
        g_copies[k - 1].wait_recv()
        summed = summed + grecv[k].astype(F32)
    factor = row_weight * (inv[:, :1] * scale)
    for g in range(per_tile):
        kg_ref[g * short:(g + 1) * short, :] = (
            summed[:, g * width:(g + 1) * width] * factor[g * short:(g + 1) * short])
    for copy in g_copies:
        copy.wait_send()


def local(n_var, n_dp, fields, kernels, level_map, norm_gain_vector, w_in, w_out, cotangent):
    batch, vars_local, height, across = fields.shape
    hp, wp = height // PATCH, across // PATCH
    features, hidden_units = w_in.shape
    levels, rows = cotangent.shape[1:3]
    width = features // n_dp
    scale = float(batch * n_dp * hp * wp) ** (-0.5)
    pp = PATCH * PATCH
    lines = vars_local * height
    short = vars_local * pp * width // LANES
    g_type = BF16 if short % 16 == 0 else F32
    tokens_all = hp * wp
    any_spec = pl.BlockSpec(memory_space=pl.ANY)
    dma = pltpu.SemaphoreType.DMA
    out, grad = pl.pallas_call(
        functools.partial(kernel, n_var, n_dp, width, scale, vars_local, wp, hp),
        out_shape=(
            jax.ShapeDtypeStruct((levels, rows, features), BF16),
            jax.ShapeDtypeStruct((vars_local * pp, width), F32),
        ),
        in_specs=[pl.BlockSpec(memory_space=pltpu.SMEM)] + [any_spec] * 6,
        out_specs=(any_spec, pl.BlockSpec(memory_space=pltpu.VMEM)),
        scratch_shapes=[
            pltpu.VMEM((lines, across), BF16),
            pltpu.VMEM((vars_local * pp, features), BF16),
            pltpu.VMEM((1, features), F32),
            pltpu.VMEM((features, hidden_units), BF16),
            pltpu.VMEM((hidden_units, features), BF16),
            pltpu.VMEM((n_var, rows, features), BF16),
            pltpu.VMEM((n_var, rows, features), BF16),
            pltpu.VMEM((tokens_all // LANES, vars_local * pp, LANES), F32),
            pltpu.VMEM((vars_local * pp, tokens_all), BF16),
            pltpu.VMEM((tokens_all, hidden_units), F32),
            pltpu.VMEM((n_dp, short, LANES), g_type),
            pltpu.VMEM((n_dp, short, LANES), g_type),
            dma((3,)), dma((CHUNKS,)), dma((CHUNKS,)),
            dma((n_var,)), dma((n_var,)), dma((2,)),
            dma((n_var,)), dma((n_var,)), dma((n_dp,)), dma((n_dp,)),
        ],
        compiler_params=pltpu.CompilerParams(
            collective_id=0, has_side_effects=True, vmem_limit_bytes=58 * 1024 * 1024),
    )(
        level_map,
        fields.reshape(lines, across),
        kernels.reshape(vars_local * pp, features),
        norm_gain_vector.reshape(1, features),
        w_in, w_out,
        cotangent.reshape(levels, rows, features),
    )
    return out.reshape(cotangent.shape), grad.reshape(vars_local, pp, width)


def solution(mesh):
    placed = (
        P("dp", "var", None, None),
        P("var", None, None),
        P("var"),
        P(),
        P(),
        P(),
        P("dp", None, "var", None),
    )
    return jax.shard_map(
        functools.partial(local, mesh.shape["var"], mesh.shape["dp"]),
        mesh=mesh,
        in_specs=placed,
        out_specs=(P("dp", None, "var", None), P("var", None, "dp")),
        check_vma=False,
    )
```

```python
import functools

import jax
import jax.numpy as jnp
from jax import lax
from jax.experimental import pallas as pl
from jax.experimental.pallas import tpu as pltpu
from jax.sharding import PartitionSpec as P

PATCH = 4
LANES = 128
CHUNKS = 4
MESH = pl.DeviceIdType.MESH
F32 = jnp.float32
BF16 = jnp.bfloat16
GELU_C = 0.7978845608028654
GELU_A = 0.044715


def dot_nn(a, b):
    return lax.dot_general(a, b, (((1,), (0,)), ((), ())), preferred_element_type=F32)


def dot_nt(a, b):
    return lax.dot_general(a, b, (((1,), (1,)), ((), ())), preferred_element_type=F32)


def dot_tn(a, b):
    return lax.dot_general(a, b, (((0,), (0,)), ((), ())), preferred_element_type=F32)


def kernel(
    n_var, n_dp, width, scale, vars_local, wp, hp,
    map_hbm, fields_hbm, kernels_hbm, gain_hbm, win_hbm, wout_hbm, cot_hbm,
    out_hbm, kg_ref,
    map_ref, fields_v, kernels_v, gain_v, win, wout, cot_all, out_all,
    patch32, patch, gprime, gsend, grecv,
    in_sem, win_sem, wout_sem, cot_send, cot_recv, own_sem,
    out_send, out_recv, g_send, g_recv,
):
    my_var = lax.axis_index("var")
    my_dp = lax.axis_index("dp")
    features, hidden_units = win.shape
    step = hidden_units // CHUNKS
    rows = cot_all.shape[1]
    tokens_all = n_var * rows

    barrier = pltpu.get_barrier_semaphore()
    for k in range(1, n_var):
        pl.semaphore_signal(barrier, inc=1, device_id={"var": lax.rem(my_var + k, n_var)}, device_id_type=MESH)
    for k in range(1, n_dp):
        pl.semaphore_signal(barrier, inc=1, device_id={"dp": lax.rem(my_dp + k, n_dp)}, device_id_type=MESH)

    small = [
        pltpu.make_async_copy(fields_hbm, fields_v, in_sem.at[0]),
        pltpu.make_async_copy(kernels_hbm, kernels_v, in_sem.at[1]),
        pltpu.make_async_copy(gain_hbm, gain_v, in_sem.at[2]),
        pltpu.make_async_copy(map_hbm, map_ref, in_sem.at[3]),
    ]
    for copy in small:
        copy.start()
    win_copies, wout_copies = [], []
    for c in range(CHUNKS):
        part = pl.ds(c * step, step)
        win_copies.append(pltpu.make_async_copy(win_hbm.at[:, part], win.at[:, part], win_sem.at[c]))
        wout_copies.append(pltpu.make_async_copy(wout_hbm.at[part], wout.at[part], wout_sem.at[c]))
        win_copies[c].start()
        wout_copies[c].start()

    pl.semaphore_wait(barrier, n_var - 1 + n_dp - 1)

    cot_copies = []
    for k in range(1, n_var):
        dest = lax.rem(my_var + k, n_var)
        cot_copies.append(pltpu.make_async_remote_copy(
            src_ref=cot_hbm.at[dest], dst_ref=cot_all.at[my_var],
            send_sem=cot_send.at[k], recv_sem=cot_recv.at[k],
            device_id={"var": dest}, device_id_type=MESH))
        cot_copies[-1].start()
    own_cot = pltpu.make_async_copy(cot_hbm.at[my_var], cot_all.at[my_var], own_sem.at[0])
    own_cot.start()

    small[0].wait()
    lines = fields_v.shape[0]
    group = LANES // wp
    per_hp = lines // hp
    r_id = lax.broadcasted_iota(jnp.int32, (LANES, LANES), 0)
    c_id = lax.broadcasted_iota(jnp.int32, (LANES, LANES), 1)
    pick = (r_id == PATCH * (c_id % wp) + c_id // wp).astype(BF16)
    o_id = lax.broadcasted_iota(jnp.int32, (lines, lines), 0)
    i_id = lax.broadcasted_iota(jnp.int32, (lines, lines), 1)
    order = (
        i_id == (hp * PATCH) * ((o_id // PATCH) % vars_local) + PATCH * (o_id // per_hp) + o_id % PATCH
    ).astype(BF16)
    spread = dot_nn(order, dot_nn(fields_v[...], pick).astype(BF16))
    lane_group = lax.broadcasted_iota(jnp.int32, (per_hp, LANES), 1) // wp
    for t in range(hp // group):
        for j in range(PATCH):
            block = None
            for g in range(group):
                source = spread[(group * t + g) * per_hp:(group * t + g + 1) * per_hp, :]
                shift = (wp * (g - j)) % LANES
                moved = pltpu.roll(source, shift, 1) if shift else source
                block = moved if block is None else jnp.where(lane_group == g, moved, block)
            patch32[t, pl.ds(j, per_hp, stride=PATCH), :] = block
        patch[:, t * LANES:(t + 1) * LANES] = patch32[t].astype(BF16)

    small[3].wait()
    weights = [map_ref[v].astype(F32) for v in range(vars_local)]
    count = weights[0]
    for v in range(1, vars_local):
        count = count + weights[v]
    pp = PATCH * PATCH
    inv = 1.0 / jnp.maximum(jnp.full((1, features), count, F32), 1.0)
    row_var = lax.broadcasted_iota(jnp.int32, (vars_local * pp, 1), 0) // pp
    row_weight = jnp.zeros((vars_local * pp, 1), F32)
    for v in range(vars_local):
        row_weight = jnp.where(row_var == v, weights[v], row_weight)
    small[1].wait()
    chosen = (kernels_v[...].astype(F32) * row_weight).astype(BF16)
    tokens = (dot_tn(patch[...], chosen) * inv).astype(BF16).astype(F32)
    mean = jnp.mean(tokens, axis=1, keepdims=True)
    centered = tokens - mean
    rstd = lax.rsqrt(jnp.mean(centered * centered, axis=1, keepdims=True) + 1e-5)
    xhat = centered * rstd
    small[2].wait()
    gain = gain_v[...]
    normed = (xhat * gain).astype(BF16)

    total = tokens
    for c in range(CHUNKS):
        win_copies[c].wait()
        pre = dot_nn(normed, win[:, c * step:(c + 1) * step])
        sq = pre * pre
        half = 0.5 + 0.5 * jnp.tanh(pre * (GELU_C + (GELU_C * GELU_A) * sq))
        hid = pre * half
        gprime[:, c * step:(c + 1) * step] = half + hid * (1.0 - half) * (
            2.0 * GELU_C + (6.0 * GELU_C * GELU_A) * sq)
        wout_copies[c].wait()
        total = total + dot_nn(hid.astype(BF16), wout[c * step:(c + 1) * step, :])
    out_all[...] = total.astype(BF16).reshape(n_var, rows, features)

    out_copies = []
    for k in range(1, n_var):
        dest = lax.rem(my_var + k, n_var)
        out_copies.append(pltpu.make_async_remote_copy(
            src_ref=out_all.at[dest], dst_ref=out_hbm.at[my_var],
            send_sem=out_send.at[k], recv_sem=out_recv.at[k],
            device_id={"var": dest}, device_id_type=MESH))
        out_copies[-1].start()
    own_out = pltpu.make_async_copy(out_all.at[my_var], out_hbm.at[my_var], own_sem.at[1])
    own_out.start()

    own_cot.wait()
    for copy in cot_copies:
        copy.wait()
    cot = cot_all[...].reshape(tokens_all, features)
    dnorm = None
    for c in range(CHUNKS):
        dhid = dot_nt(cot, wout[c * step:(c + 1) * step, :])
        dpre = (dhid * gprime[:, c * step:(c + 1) * step]).astype(BF16)
        term = dot_nt(dpre, win[:, c * step:(c + 1) * step])
        dnorm = term if dnorm is None else dnorm + term
    dx = dnorm * gain
    dtok = cot.astype(F32) + rstd * (
        dx - jnp.mean(dx, axis=1, keepdims=True)
        - xhat * jnp.mean(dx * xhat, axis=1, keepdims=True))
    grad = dot_nn(patch[...], dtok.astype(BF16))

    per_tile = LANES // width
    short = grad.shape[0] // per_tile
    lane_part = lax.broadcasted_iota(jnp.int32, (short, LANES), 1) // width
    for d in range(n_dp):
        tile, j = d // per_tile, d % per_tile
        packed = None
        for g in range(per_tile):
            source = grad[g * short:(g + 1) * short, tile * LANES:(tile + 1) * LANES]
            shift = (width * (g - j)) % LANES
            moved = pltpu.roll(source, shift, 1) if shift else source
            packed = moved if packed is None else jnp.where(lane_part == g, moved, packed)
        gsend[d] = packed.astype(gsend.dtype)
    g_copies = []
    for k in range(1, n_dp):
        dest = lax.rem(my_dp + k, n_dp)
        g_copies.append(pltpu.make_async_remote_copy(
            src_ref=gsend.at[dest], dst_ref=grecv.at[k],
            send_sem=g_send.at[k], recv_sem=g_recv.at[k],
            device_id={"dp": dest}, device_id_type=MESH))
        g_copies[-1].start()
    own_out.wait()
    for copy in out_copies:
        copy.wait()
    summed = gsend[my_dp].astype(F32)
    for k in range(1, n_dp):
        g_copies[k - 1].wait_recv()
        summed = summed + grecv[k].astype(F32)
    factor = row_weight * (inv[:, :1] * scale)
    for g in range(per_tile):
        kg_ref[g * short:(g + 1) * short, :] = (
            summed[:, g * width:(g + 1) * width] * factor[g * short:(g + 1) * short])
    for copy in g_copies:
        copy.wait_send()


def local(n_var, n_dp, fields, kernels, level_map, norm_gain_vector, w_in, w_out, cotangent):
    batch, vars_local, height, across = fields.shape
    hp, wp = height // PATCH, across // PATCH
    features, hidden_units = w_in.shape
    levels, rows = cotangent.shape[1:3]
    width = features // n_dp
    scale = float(batch * n_dp * hp * wp) ** (-0.5)
    pp = PATCH * PATCH
    lines = vars_local * height
    short = vars_local * pp * width // LANES
    g_type = BF16 if short % 16 == 0 else F32
    tokens_all = hp * wp
    any_spec = pl.BlockSpec(memory_space=pl.ANY)
    dma = pltpu.SemaphoreType.DMA
    out, grad = pl.pallas_call(
        functools.partial(kernel, n_var, n_dp, width, scale, vars_local, wp, hp),
        out_shape=(
            pltpu.VMEM((levels, rows, features), BF16),
            pltpu.VMEM((vars_local * pp, width), F32),
        ),
        in_specs=[any_spec] * 7,
        out_specs=(any_spec, pl.BlockSpec(memory_space=pltpu.VMEM)),
        scratch_shapes=[
            pltpu.SMEM((vars_local,), jnp.int32),
            pltpu.VMEM((lines, across), BF16),
            pltpu.VMEM((vars_local * pp, features), BF16),
            pltpu.VMEM((1, features), F32),
            pltpu.VMEM((features, hidden_units), BF16),
            pltpu.VMEM((hidden_units, features), BF16),
            pltpu.VMEM((n_var, rows, features), BF16),
            pltpu.VMEM((n_var, rows, features), BF16),
            pltpu.VMEM((tokens_all // LANES, vars_local * pp, LANES), F32),
            pltpu.VMEM((vars_local * pp, tokens_all), BF16),
            pltpu.VMEM((tokens_all, hidden_units), F32),
            pltpu.VMEM((n_dp, short, LANES), g_type),
            pltpu.VMEM((n_dp, short, LANES), g_type),
            dma((4,)), dma((CHUNKS,)), dma((CHUNKS,)),
            dma((n_var,)), dma((n_var,)), dma((2,)),
            dma((n_var,)), dma((n_var,)), dma((n_dp,)), dma((n_dp,)),
        ],
        compiler_params=pltpu.CompilerParams(
            collective_id=0, has_side_effects=True, vmem_limit_bytes=58 * 1024 * 1024),
    )(
        level_map,
        fields.reshape(lines, across),
        kernels.reshape(vars_local * pp, features),
        norm_gain_vector.reshape(1, features),
        w_in, w_out,
        cotangent.reshape(levels, rows, features),
    )
    return out.reshape(cotangent.shape), grad.reshape(vars_local, pp, width)


def solution(mesh):
    placed = (
        P("dp", "var", None, None),
        P("var", None, None),
        P("var"),
        P(),
        P(),
        P(),
        P("dp", None, "var", None),
    )
    return jax.shard_map(
        functools.partial(local, mesh.shape["var"], mesh.shape["dp"]),
        mesh=mesh,
        in_specs=placed,
        out_specs=(P("dp", None, "var", None), P("var", None, "dp")),
        check_vma=False,
    )
```

```python
import functools

import jax
import jax.numpy as jnp
from jax import lax
from jax.experimental import pallas as pl
from jax.experimental.pallas import tpu as pltpu
from jax.sharding import PartitionSpec as P

PATCH = 4
LANES = 128
CHUNKS = 1
MESH = pl.DeviceIdType.MESH
F32 = jnp.float32
BF16 = jnp.bfloat16
GELU_C = 0.7978845608028654
GELU_A = 0.044715


def dot_nn(a, b):
    return lax.dot_general(a, b, (((1,), (0,)), ((), ())), preferred_element_type=F32)


def dot_nt(a, b):
    return lax.dot_general(a, b, (((1,), (1,)), ((), ())), preferred_element_type=F32)


def dot_tn(a, b):
    return lax.dot_general(a, b, (((0,), (0,)), ((), ())), preferred_element_type=F32)


def kernel(
    n_var, n_dp, width, scale, vars_local, wp, hp,
    map_hbm, fields_hbm, kernels_hbm, gain_hbm, win_hbm, wout_hbm, cot_hbm,
    out_hbm, kg_ref,
    map_ref, fields_v, kernels_v, gain_v, win, wout, cot_all, out_all,
    patch32, patch, gprime, gsend, grecv,
    in_sem, win_sem, wout_sem, cot_send, cot_recv, own_sem,
    out_send, out_recv, g_send, g_recv,
):
    my_var = lax.axis_index("var")
    my_dp = lax.axis_index("dp")
    features, hidden_units = win.shape
    step = hidden_units // CHUNKS
    rows = cot_all.shape[1]
    tokens_all = n_var * rows

    barrier = pltpu.get_barrier_semaphore()
    for k in range(1, n_var):
        pl.semaphore_signal(barrier, inc=1, device_id={"var": lax.rem(my_var + k, n_var)}, device_id_type=MESH)
    for k in range(1, n_dp):
        pl.semaphore_signal(barrier, inc=1, device_id={"dp": lax.rem(my_dp + k, n_dp)}, device_id_type=MESH)

    small = [
        pltpu.make_async_copy(fields_hbm, fields_v, in_sem.at[0]),
        pltpu.make_async_copy(kernels_hbm, kernels_v, in_sem.at[1]),
        pltpu.make_async_copy(gain_hbm, gain_v, in_sem.at[2]),
        pltpu.make_async_copy(map_hbm, map_ref, in_sem.at[3]),
    ]
    for copy in small:
        copy.start()
    win_copies, wout_copies = [], []
    for c in range(CHUNKS):
        part = pl.ds(c * step, step)
        win_copies.append(pltpu.make_async_copy(win_hbm.at[:, part], win.at[:, part], win_sem.at[c]))
        wout_copies.append(pltpu.make_async_copy(wout_hbm.at[part], wout.at[part], wout_sem.at[c]))
        win_copies[c].start()
        wout_copies[c].start()

    pl.semaphore_wait(barrier, n_var - 1 + n_dp - 1)

    cot_copies = []
    for k in range(1, n_var):
        dest = lax.rem(my_var + k, n_var)
        cot_copies.append(pltpu.make_async_remote_copy(
            src_ref=cot_hbm.at[dest], dst_ref=cot_all.at[my_var],
            send_sem=cot_send.at[k], recv_sem=cot_recv.at[k],
            device_id={"var": dest}, device_id_type=MESH))
        cot_copies[-1].start()
    own_cot = pltpu.make_async_copy(cot_hbm.at[my_var], cot_all.at[my_var], own_sem.at[0])
    own_cot.start()

    small[0].wait()
    lines = fields_v.shape[0]
    group = LANES // wp
    per_hp = lines // hp
    r_id = lax.broadcasted_iota(jnp.int32, (LANES, LANES), 0)
    c_id = lax.broadcasted_iota(jnp.int32, (LANES, LANES), 1)
    pick = (r_id == PATCH * (c_id % wp) + c_id // wp).astype(BF16)
    o_id = lax.broadcasted_iota(jnp.int32, (lines, lines), 0)
    i_id = lax.broadcasted_iota(jnp.int32, (lines, lines), 1)
    order = (
        i_id == (hp * PATCH) * ((o_id // PATCH) % vars_local) + PATCH * (o_id // per_hp) + o_id % PATCH
    ).astype(BF16)
    spread = dot_nn(order, dot_nn(fields_v[...], pick).astype(BF16))
    lane_group = lax.broadcasted_iota(jnp.int32, (per_hp, LANES), 1) // wp
    for t in range(hp // group):
        for j in range(PATCH):
            block = None
            for g in range(group):
                source = spread[(group * t + g) * per_hp:(group * t + g + 1) * per_hp, :]
                shift = (wp * (g - j)) % LANES
                moved = pltpu.roll(source, shift, 1) if shift else source
                block = moved if block is None else jnp.where(lane_group == g, moved, block)
            patch32[t, pl.ds(j, per_hp, stride=PATCH), :] = block
        patch[:, t * LANES:(t + 1) * LANES] = patch32[t].astype(BF16)

    small[3].wait()
    weights = [map_ref[v].astype(F32) for v in range(vars_local)]
    count = weights[0]
    for v in range(1, vars_local):
        count = count + weights[v]
    pp = PATCH * PATCH
    inv = 1.0 / jnp.maximum(jnp.full((1, features), count, F32), 1.0)
    row_var = lax.broadcasted_iota(jnp.int32, (vars_local * pp, 1), 0) // pp
    row_weight = jnp.zeros((vars_local * pp, 1), F32)
    for v in range(vars_local):
        row_weight = jnp.where(row_var == v, weights[v], row_weight)
    small[1].wait()
    chosen = (kernels_v[...].astype(F32) * row_weight).astype(BF16)
    tokens = (dot_tn(patch[...], chosen) * inv).astype(BF16).astype(F32)
    mean = jnp.mean(tokens, axis=1, keepdims=True)
    centered = tokens - mean
    rstd = lax.rsqrt(jnp.mean(centered * centered, axis=1, keepdims=True) + 1e-5)
    xhat = centered * rstd
    small[2].wait()
    gain = gain_v[...]
    normed = (xhat * gain).astype(BF16)

    for copy in win_copies + wout_copies:
        copy.wait()
    total = tokens
    for c in range(CHUNKS):
        pre = dot_nn(normed, win[:, c * step:(c + 1) * step])
        sq = pre * pre
        half = 0.5 + 0.5 * jnp.tanh(pre * (GELU_C + (GELU_C * GELU_A) * sq))
        hid = pre * half
        gprime[:, c * step:(c + 1) * step] = half + hid * (1.0 - half) * (
            2.0 * GELU_C + (6.0 * GELU_C * GELU_A) * sq)
        total = total + dot_nn(hid.astype(BF16), wout[c * step:(c + 1) * step, :])
    out_all[...] = total.astype(BF16).reshape(n_var, rows, features)

    out_copies = []
    for k in range(1, n_var):
        dest = lax.rem(my_var + k, n_var)
        out_copies.append(pltpu.make_async_remote_copy(
            src_ref=out_all.at[dest], dst_ref=out_hbm.at[my_var],
            send_sem=out_send.at[k], recv_sem=out_recv.at[k],
            device_id={"var": dest}, device_id_type=MESH))
        out_copies[-1].start()
    own_out = pltpu.make_async_copy(out_all.at[my_var], out_hbm.at[my_var], own_sem.at[1])
    own_out.start()

    own_cot.wait()
    for copy in cot_copies:
        copy.wait()
    cot = cot_all[...].reshape(tokens_all, features)
    dnorm = None
    for c in range(CHUNKS):
        dhid = dot_nt(cot, wout[c * step:(c + 1) * step, :])
        dpre = (dhid * gprime[:, c * step:(c + 1) * step]).astype(BF16)
        term = dot_nt(dpre, win[:, c * step:(c + 1) * step])
        dnorm = term if dnorm is None else dnorm + term
    dx = dnorm * gain
    dtok = cot.astype(F32) + rstd * (
        dx - jnp.mean(dx, axis=1, keepdims=True)
        - xhat * jnp.mean(dx * xhat, axis=1, keepdims=True))
    grad = dot_nn(patch[...], dtok.astype(BF16))

    per_tile = LANES // width
    short = grad.shape[0] // per_tile
    lane_part = lax.broadcasted_iota(jnp.int32, (short, LANES), 1) // width
    for d in range(n_dp):
        tile, j = d // per_tile, d % per_tile
        packed = None
        for g in range(per_tile):
            source = grad[g * short:(g + 1) * short, tile * LANES:(tile + 1) * LANES]
            shift = (width * (g - j)) % LANES
            moved = pltpu.roll(source, shift, 1) if shift else source
            packed = moved if packed is None else jnp.where(lane_part == g, moved, packed)
        gsend[d] = packed.astype(gsend.dtype)
    g_copies = []
    for k in range(1, n_dp):
        dest = lax.rem(my_dp + k, n_dp)
        g_copies.append(pltpu.make_async_remote_copy(
            src_ref=gsend.at[dest], dst_ref=grecv.at[k],
            send_sem=g_send.at[k], recv_sem=g_recv.at[k],
            device_id={"dp": dest}, device_id_type=MESH))
        g_copies[-1].start()
    own_out.wait()
    for copy in out_copies:
        copy.wait()
    summed = gsend[my_dp].astype(F32)
    for k in range(1, n_dp):
        g_copies[k - 1].wait_recv()
        summed = summed + grecv[k].astype(F32)
    factor = row_weight * (inv[:, :1] * scale)
    for g in range(per_tile):
        kg_ref[g * short:(g + 1) * short, :] = (
            summed[:, g * width:(g + 1) * width] * factor[g * short:(g + 1) * short])
    for copy in g_copies:
        copy.wait_send()


def local(n_var, n_dp, fields, kernels, level_map, norm_gain_vector, w_in, w_out, cotangent):
    batch, vars_local, height, across = fields.shape
    hp, wp = height // PATCH, across // PATCH
    features, hidden_units = w_in.shape
    levels, rows = cotangent.shape[1:3]
    width = features // n_dp
    scale = float(batch * n_dp * hp * wp) ** (-0.5)
    pp = PATCH * PATCH
    lines = vars_local * height
    short = vars_local * pp * width // LANES
    g_type = BF16 if short % 16 == 0 else F32
    tokens_all = hp * wp
    any_spec = pl.BlockSpec(memory_space=pl.ANY)
    dma = pltpu.SemaphoreType.DMA
    out, grad = pl.pallas_call(
        functools.partial(kernel, n_var, n_dp, width, scale, vars_local, wp, hp),
        out_shape=(
            pltpu.VMEM((levels, rows, features), BF16),
            pltpu.VMEM((vars_local * pp, width), F32),
        ),
        in_specs=[any_spec] * 7,
        out_specs=(any_spec, pl.BlockSpec(memory_space=pltpu.VMEM)),
        scratch_shapes=[
            pltpu.SMEM((vars_local,), jnp.int32),
            pltpu.VMEM((lines, across), BF16),
            pltpu.VMEM((vars_local * pp, features), BF16),
            pltpu.VMEM((1, features), F32),
            pltpu.VMEM((features, hidden_units), BF16),
            pltpu.VMEM((hidden_units, features), BF16),
            pltpu.VMEM((n_var, rows, features), BF16),
            pltpu.VMEM((n_var, rows, features), BF16),
            pltpu.VMEM((tokens_all // LANES, vars_local * pp, LANES), F32),
            pltpu.VMEM((vars_local * pp, tokens_all), BF16),
            pltpu.VMEM((tokens_all, hidden_units), F32),
            pltpu.VMEM((n_dp, short, LANES), g_type),
            pltpu.VMEM((n_dp, short, LANES), g_type),
            dma((4,)), dma((CHUNKS,)), dma((CHUNKS,)),
            dma((n_var,)), dma((n_var,)), dma((2,)),
            dma((n_var,)), dma((n_var,)), dma((n_dp,)), dma((n_dp,)),
        ],
        compiler_params=pltpu.CompilerParams(
            collective_id=0, has_side_effects=True, vmem_limit_bytes=58 * 1024 * 1024),
    )(
        level_map,
        fields.reshape(lines, across),
        kernels.reshape(vars_local * pp, features),
        norm_gain_vector.reshape(1, features),
        w_in, w_out,
        cotangent.reshape(levels, rows, features),
    )
    return out.reshape(cotangent.shape), grad.reshape(vars_local, pp, width)


def solution(mesh):
    placed = (
        P("dp", "var", None, None),
        P("var", None, None),
        P("var"),
        P(),
        P(),
        P(),
        P("dp", None, "var", None),
    )
    return jax.shard_map(
        functools.partial(local, mesh.shape["var"], mesh.shape["dp"]),
        mesh=mesh,
        in_specs=placed,
        out_specs=(P("dp", None, "var", None), P("var", None, "dp")),
        check_vma=False,
    )
```
